32 devices in a mesh: row: 8 (over y, x, core), rep: 4 (over z).
Axes of the slice: x: 2, y: 2, z: 4, core: 2. Of those that a mesh axis runs over, the one named last changes fastest.
Arguments:
- features: bfloat16 [4096, 128], P('row'), may hold values from -6 to 6
- tiles: bfloat16 [512, 4, 256, 256], P('row', 'rep'), may hold values from -0.375 to 0.375
- tile_where: int32 [512, 4, 2], P('row', 'rep'), may hold values from 0 to 15, as said below
- tile_count: int32 [8, 4], P('row', 'rep'), may hold values from 1 to 64, as said below
- degree: int32 [4096], P('row'), may hold values from 1 to 8
- self_one: bfloat16 [128, 256], replicated, may hold values from -0.5 to 0.5
- neigh_one: bfloat16 [128, 256], replicated, may hold values from -0.5 to 0.5
- self_two: bfloat16 [256, 256], replicated, may hold values from -0.375 to 0.375
- neigh_two: bfloat16 [256, 256], replicated, may hold values from -0.375 to 0.375
Outputs:
- embedding: float32 [4096, 256], P('row')
The draws below stay inside these ranges and needn't reach their ends.
Inputs may be any that keep to these rules, and one draw needn't show every extreme that they name: `tile_where`: column 0 is a tile row of 0 to 1, column 1 a tile column of 0 to 15. `tile_count`: some block row and replica has all 64 slots live in every draw.
All inputs are finite; a program needn't handle non-finite values.
Results may differ from the reference program's by a relative error of at most 0.005.
Values may be sent and summed in bfloat16 or wider, within the bound.
A program may use at most 128 MiB of HBM per device.

```python
import jax
import jax.numpy as jnp
from jax import lax

FIN = 128
HID = 256
TILE = 256
ROWS_DEV = 512
SLOTS = 64
NODES = 4096
N_ROW = 8
N_REP = 4


def draw_tile_where(key, part):
    total_rows = NODES // ROWS_DEV * SLOTS
    key_rows = jax.random.fold_in(key, 11)
    key_cols = jax.random.fold_in(key, 12)
    tile_rows = jax.random.randint(key_rows, (total_rows, N_REP, 1), 0, ROWS_DEV // TILE, dtype=jnp.int32)
    tile_cols = jax.random.randint(key_cols, (total_rows, N_REP, 1), 0, NODES // TILE, dtype=jnp.int32)
    return jnp.concatenate([tile_rows, tile_cols], axis=2)


def draw_tile_count(key, part):
    blocks = NODES // ROWS_DEV
    key_base = jax.random.fold_in(key, 21)
    key_heavy = jax.random.fold_in(key, 22)
    key_full = jax.random.fold_in(key, 23)
    base = jax.random.randint(key_base, (blocks, N_REP), max(1, SLOTS // 2), SLOTS + 1, dtype=jnp.int32)
    heavy = jax.random.randint(key_heavy, (blocks, N_REP), 0, 8, dtype=jnp.int32) == 0
    counts = jnp.where(heavy, SLOTS, base)
    chosen = jax.random.randint(key_full, (), 0, blocks * N_REP, dtype=jnp.int32)
    places = jnp.arange(blocks * N_REP, dtype=jnp.int32).reshape(blocks, N_REP)
    return jnp.where(places == chosen, SLOTS, counts).astype(jnp.int32)


def with_ends(entries, rng, least, high):
    dims = entries.shape
    place = [jax.random.randint(jax.random.fold_in(rng, axis), (), 0, dims[axis]) for axis in range(len(dims))]
    entries = entries.at[tuple(place)].set(least)
    longest = dims.index(max(dims))
    place[longest] = (place[longest] + 1) % dims[longest]
    return entries.at[tuple(place)].set(high)


def levels(own_key, shape, shards, least, high):
    level, own = 1.0, jax.random.fold_in(own_key, 6)
    for axis_at, blocks in shards:
        steps = jnp.exp(jax.random.uniform(jax.random.fold_in(own, axis_at), (blocks,), jnp.float32, least / len(shards), high / len(shards)))
        level = level * jnp.repeat(steps, shape[axis_at] // blocks).reshape([-1 if axis == axis_at else 1 for axis in range(len(shape))])
    return level


def centred(key, dims, spread, reach, pieces=(), held_as=jnp.bfloat16):
    gain = levels(key, dims, pieces, -0.22, 0.18) if pieces else 1.0
    drawn = jax.random.normal(key, dims, jnp.float32) * spread * gain
    return jnp.minimum(jnp.maximum(drawn, -reach), reach).astype(held_as)


def setup_inputs(seed: int = 0) -> dict:
    streams_of = jax.random.split(jax.random.key(seed), 10)
    features = centred(streams_of[0], (NODES, FIN), 1.0, 6.0, ((0, 8),))
    tiles = centred(streams_of[1], (N_ROW * SLOTS, N_REP, TILE, TILE), TILE ** -0.5, 0.375, ((0, 8), (1, 4)))
    tile_where = draw_tile_where(jax.random.fold_in(streams_of[9], 71), 0)
    tile_count = draw_tile_count(jax.random.fold_in(streams_of[9], 71), 0)
    degree = with_ends(jax.random.randint(streams_of[4], (NODES,), 1, 9), jax.random.fold_in(streams_of[4], 1), 1, 8).astype(jnp.int32)
    self_one = centred(streams_of[5], (FIN, HID), FIN ** -0.5, 0.5)
    neigh_one = centred(streams_of[6], (FIN, HID), FIN ** -0.5, 0.5)
    self_two = centred(streams_of[7], (HID, HID), HID ** -0.5, 0.375)
    neigh_two = centred(streams_of[8], (HID, HID), HID ** -0.5, 0.375)
    return dict(features=features, tiles=tiles, tile_where=tile_where, tile_count=tile_count, degree=degree, self_one=self_one, neigh_one=neigh_one, self_two=self_two, neigh_two=neigh_two)


def adjacency_product(values, tiles, tile_where, tile_count):
    width = values.shape[1]
    per_block = ROWS_DEV // TILE
    blocks = values.reshape(-1, TILE, width)
    tiles_all = tiles.reshape(N_ROW, SLOTS, N_REP, TILE, TILE)
    where_all = tile_where.reshape(N_ROW, SLOTS, N_REP, 2)

    def one_row(operands):
        tile_block, where_block, count_block = operands
        columns = jnp.take(blocks, where_block[..., 1], axis=0)
        products = jnp.einsum('scij,scjf->scif', tile_block.astype(jnp.float32), columns.astype(jnp.float32), precision=lax.Precision.HIGHEST)
        live = jnp.arange(SLOTS, dtype=jnp.int32)[:, None] < count_block[None, :]
        placing = (where_block[..., 0][..., None] == jnp.arange(per_block, dtype=jnp.int32)) & live[..., None]
        summed = jnp.einsum('sct,scif->tif', placing.astype(jnp.float32), products, precision=lax.Precision.HIGHEST)
        return summed.reshape(ROWS_DEV, width)

    partial_value = lax.map(one_row, (tiles_all, where_all, tile_count))
    return partial_value.reshape(-1, width)


def reference(features, tiles, tile_where, tile_count, degree, self_one, neigh_one, self_two, neigh_two):
    scale = degree.astype(jnp.float32)[:, None]
    agg_one = (adjacency_product(features, tiles, tile_where, tile_count) / scale).astype(jnp.bfloat16)
    first = jnp.dot(features, self_one, preferred_element_type=jnp.float32) + jnp.dot(agg_one, neigh_one, preferred_element_type=jnp.float32)
    hidden = jax.nn.relu(first).astype(jnp.bfloat16)
    agg_two = (adjacency_product(hidden, tiles, tile_where, tile_count) / scale).astype(jnp.bfloat16)
    return jnp.dot(hidden, self_two, preferred_element_type=jnp.float32) + jnp.dot(agg_two, neigh_two, preferred_element_type=jnp.float32)
```

```python
import functools

import jax
import jax.numpy as jnp
from jax import lax
from jax.experimental import pallas as pl
from jax.experimental.pallas import tpu as pltpu
from jax.sharding import PartitionSpec as P

GROUP = 4
MESH = pl.DeviceIdType.MESH
F32 = jnp.float32
BF16 = jnp.bfloat16


def kernel(
    n_row, n_rep,
    where, mask, degree, features, tiles, self_one, neigh_one, self_two, neigh_two,
    out,
    tile_v, feat_v, share_v, w_self1, w_neigh1, w_self2, w_neigh2,
    acc1, send1, recv1, hid_v, acc2, send2, recv2, out_v,
    local_sem, f_send, f_recv, p1_send, p1_recv, h_send, h_recv, p2_send, p2_recv, o_send, o_recv,
):
    slots, tile, _ = tile_v.shape
    per_block, _, width_in = features.shape
    rows = per_block * tile
    quarter = rows // n_rep
    per_tile = tile // quarter
    chips = n_row // 2
    row, rep = lax.axis_index("row"), lax.axis_index("rep")
    chip, core = lax.div(row, 2), lax.rem(row, 2)
    sibling = chip * 2 + 1 - core
    others = [lax.rem(chip + k, chips) * 2 + core for k in range(1, chips)]
    others_sib = [lax.rem(chip + k, chips) * 2 + 1 - core for k in range(1, chips)]
    reps = [lax.rem(rep + k, n_rep) for k in range(1, n_rep)]
    reps_from = [lax.rem(rep + n_rep - k, n_rep) for k in range(1, n_rep)]

    pending = []

    def local(src, dst, sem):
        copy = pltpu.make_async_copy(src, dst, local_sem.at[sem])
        copy.start()
        return copy

    tile_copy = local(tiles, tile_v, 0)
    share_copy = local(
        features.at[lax.div(rep, per_tile), pl.ds(pl.multiple_of(lax.rem(rep, per_tile) * quarter, quarter), quarter)],
        share_v, 1,
    )
    own_copy = local(features, feat_v.at[pl.ds(row * per_block, per_block)], 2)
    w_copies = [
        local(src, dst, 3 + n)
        for n, (src, dst) in enumerate(
            ((self_one, w_self1), (neigh_one, w_neigh1), (self_two, w_self2), (neigh_two, w_neigh2))
        )
    ]

    barrier = pltpu.get_barrier_semaphore()
    peers = [(r, rep) for r in others + [sibling]] + [(row, q) for q in reps]
    for peer in peers:
        pl.semaphore_signal(barrier, inc=1, device_id=peer, device_id_type=MESH)
    pl.semaphore_wait(barrier, len(peers))

    def remote(src, dst, send, recv, to):
        copy = pltpu.make_async_remote_copy(
            src_ref=src, dst_ref=dst, send_sem=send, recv_sem=recv, device_id=to, device_id_type=MESH
        )
        copy.start()
        pending.append(copy)
        return copy

    def arrived(ref, send, recv):
        pltpu.make_async_remote_copy(
            src_ref=ref, dst_ref=ref, send_sem=send, recv_sem=recv, device_id=(sibling, rep), device_id_type=MESH
        ).wait_recv()

    def feat_at(r):
        return feat_v.at[pl.ds(r * per_block, per_block)]

    for k, r in enumerate(others):
        remote(features, feat_at(row), f_send.at[k], f_recv.at[row], (r, rep))
    remote(features, feat_at(row), f_send.at[chips - 1], f_recv.at[row], (sibling, rep))
    for k, r in enumerate(others):
        arrived(feat_at(r), f_send.at[0], f_recv.at[r])
        remote(feat_at(r), feat_at(r), f_send.at[chips + k], f_recv.at[r], (sibling, rep))

    acc1[...] = jnp.zeros_like(acc1)
    share_copy.wait()
    for copy in w_copies:
        copy.wait()
    first = jnp.dot(share_v[...], w_self1[...], preferred_element_type=F32)
    counts = jnp.broadcast_to(degree[pl.ds(rep, 1), :].astype(F32), (quarter, quarter))
    eye = lax.broadcasted_iota(jnp.int32, (quarter, quarter), 0) == lax.broadcasted_iota(
        jnp.int32, (quarter, quarter), 1
    )
    scale = jnp.sum(jnp.where(eye, counts, 0.0), axis=1, keepdims=True)
    own_copy.wait()
    tile_copy.wait()
    arrived(feat_at(sibling), f_send.at[0], f_recv.at[sibling])
    for r in others_sib:
        arrived(feat_at(r), f_send.at[0], f_recv.at[r])

    def product(held, acc):
        def body(g, carry):
            lhs, rhs = [], []
            for u in range(GROUP):
                s = g * GROUP + u
                block = held[where[1, s]]
                lhs.append(tile_v[s])
                rhs.append(
                    jnp.concatenate(
                        [
                            block * jnp.full((1, block.shape[1]), mask[i, s], F32).astype(BF16)
                            for i in range(per_block)
                        ],
                        axis=1,
                    )
                )
            acc[...] += jnp.dot(
                jnp.concatenate(lhs, axis=1), jnp.concatenate(rhs, axis=0), preferred_element_type=F32
            )
            return carry

        lax.fori_loop(0, slots // GROUP, body, 0)

    def reduce_over_rep(acc, send, recv, send_sem, recv_sem, width):
        for q in range(n_rep):
            i, h = q // per_tile, q % per_tile
            send[q] = acc[h * quarter : (h + 1) * quarter, i * width : (i + 1) * width].astype(BF16)
        for k, q in enumerate(reps):
            remote(send.at[q], recv.at[k], send_sem.at[k], recv_sem.at[k], (row, q))
        total = send[rep].astype(F32)
        for k in range(n_rep - 1):
            arrived(recv.at[k], send_sem.at[k], recv_sem.at[k])
            total += recv[k].astype(F32)
        return total

    product(feat_v, acc1)
    total1 = reduce_over_rep(acc1, send1, recv1, p1_send, p1_recv, width_in)
    agg1 = (total1 / scale).astype(BF16)
    first += jnp.dot(agg1, w_neigh1[...], preferred_element_type=F32)
    hidden = jnp.maximum(first, 0.0).astype(BF16)

    def share_at(r, q):
        start = pl.multiple_of(lax.rem(q, per_tile) * quarter, quarter)
        return hid_v.at[r * per_block + lax.div(q, per_tile), pl.ds(start, quarter)]

    share_at(row, rep)[...] = hidden
    for k, q in enumerate(reps):
        remote(share_at(row, rep), share_at(row, rep), h_send.at[0, k], h_recv.at[row, rep], (row, q))
    for n, q in enumerate([rep] + reps_from):
        if n:
            arrived(share_at(row, q), h_send.at[0, 0], h_recv.at[row, q])
        for k, r in enumerate(others):
            remote(share_at(row, q), share_at(row, q), h_send.at[1 + n, k], h_recv.at[row, q], (r, rep))
        remote(share_at(row, q), share_at(row, q), h_send.at[1 + n, chips - 1], h_recv.at[row, q], (sibling, rep))
    acc2[...] = jnp.zeros_like(acc2)
    result = jnp.dot(hidden, w_self2[...], preferred_element_type=F32)
    for n, q in enumerate([rep] + reps_from):
        for k, r in enumerate(others):
            arrived(share_at(r, q), h_send.at[0, 0], h_recv.at[r, q])
            remote(share_at(r, q), share_at(r, q), h_send.at[1 + n, chips + k], h_recv.at[r, q], (sibling, rep))
    for n, q in enumerate([rep] + reps_from):
        for r in [sibling] + others_sib:
            arrived(share_at(r, q), h_send.at[0, 0], h_recv.at[r, q])

    product(hid_v, acc2)
    total2 = reduce_over_rep(acc2, send2, recv2, p2_send, p2_recv, hid_v.shape[2])
    agg2 = (total2 / scale).astype(BF16)
    result += jnp.dot(agg2, w_neigh2[...], preferred_element_type=F32)
    out_v[rep] = result.astype(BF16)
    for k, q in enumerate(reps):
        remote(out_v.at[rep], out_v.at[rep], o_send.at[k], o_recv.at[rep], (row, q))
    for q in reps_from:
        arrived(out_v.at[q], o_send.at[0], o_recv.at[q])
    for q in range(n_rep):
        out[q * quarter : (q + 1) * quarter, :] = out_v[q]
    for copy in pending:
        copy.wait_send()


def per_device(
    features, tiles, tile_where, tile_count, degree, self_one, neigh_one, self_two, neigh_two
):
    n_row, n_rep = lax.axis_size("row"), lax.axis_size("rep")
    rows, width_in = features.shape
    slots, _, tile, _ = tiles.shape
    hid, width_out = self_two.shape
    per_block = rows // tile
    quarter = rows // n_rep
    chips = n_row // 2
    live = jnp.arange(slots, dtype=jnp.int32) < tile_count.reshape(())
    where = tile_where.reshape(slots, 2)
    rows_of = jnp.where(live, where[:, 0], per_block)
    mask = (rows_of == jnp.arange(per_block, dtype=jnp.int32)[:, None]).astype(F32)
    dma = pltpu.SemaphoreType.DMA
    any_spec = pl.BlockSpec(memory_space=pl.ANY)
    vmem = pl.BlockSpec(memory_space=pltpu.VMEM)
    out = pl.pallas_call(
        functools.partial(kernel, n_row, n_rep),
        out_shape=jax.ShapeDtypeStruct((rows, width_out), BF16),
        in_specs=[pl.BlockSpec(memory_space=pltpu.SMEM)] * 2 + [vmem] + [any_spec] * 6,
        out_specs=vmem,
        scratch_shapes=[
            pltpu.VMEM((slots, tile, tile), BF16),
            pltpu.VMEM((n_row * per_block, tile, width_in), BF16),
            pltpu.VMEM((quarter, width_in), BF16),
            pltpu.VMEM(self_one.shape, BF16),
            pltpu.VMEM(neigh_one.shape, BF16),
            pltpu.VMEM(self_two.shape, BF16),
            pltpu.VMEM(neigh_two.shape, BF16),
            pltpu.VMEM((tile, per_block * width_in), F32),
            pltpu.VMEM((n_rep, quarter, width_in), BF16),
            pltpu.VMEM((n_rep - 1, quarter, width_in), BF16),
            pltpu.VMEM((n_row * per_block, tile, hid), BF16),
            pltpu.VMEM((tile, per_block * hid), F32),
            pltpu.VMEM((n_rep, quarter, hid), BF16),
            pltpu.VMEM((n_rep - 1, quarter, hid), BF16),
            pltpu.VMEM((n_rep, quarter, width_out), BF16),
            dma((7,)),
            dma((2 * chips,)),
            dma((n_row,)),
            dma((n_rep - 1,)),
            dma((n_rep - 1,)),
            dma((1 + n_rep, max(2 * chips, n_rep))),
            dma((n_row, n_rep)),
            dma((n_rep - 1,)),
            dma((n_rep - 1,)),
            dma((n_rep - 1,)),
            dma((n_rep,)),
        ],
        compiler_params=pltpu.CompilerParams(
            collective_id=0, has_side_effects=True, vmem_limit_bytes=56 * 1024 * 1024
        ),
        name="sage",
    )(
        where.T, mask, degree.reshape(n_rep, quarter), features.reshape(per_block, tile, width_in), tiles.reshape(slots, tile, tile),
        self_one, neigh_one, self_two, neigh_two,
    )
    return out.astype(F32)


def solution(mesh):
    return jax.shard_map(
        per_device,
        mesh=mesh,
        in_specs=(
            P("row", None),
            P("row", "rep", None, None),
            P("row", "rep", None),
            P("row", "rep"),
            P("row"),
            P(),
            P(),
            P(),
            P(),
        ),
        out_specs=P("row", None),
        check_vma=False,
    )
```

```python
import functools

import jax
import jax.numpy as jnp
from jax import lax
from jax.experimental import pallas as pl
from jax.experimental.pallas import tpu as pltpu
from jax.sharding import PartitionSpec as P

GROUP = 8
MESH = pl.DeviceIdType.MESH
F32 = jnp.float32
BF16 = jnp.bfloat16


def kernel(
    n_row, n_rep,
    where, count, degree, features, tiles, self_one, neigh_one, self_two, neigh_two,
    out,
    tile_v, feat_v, w_one, w_self2, w_neigh2,
    acc, send1, recv1, agg_v, hid_v, send2, recv2, out_v,
    local_sem, f_send, f_recv, p1_send, p1_recv, h_send, h_recv, p2_send, p2_recv, o_send, o_recv,
):
    slots, tile, _ = tile_v.shape
    per_block, _, width_in = features.shape
    rows = per_block * tile
    quarter = rows // n_rep
    per_tile = tile // quarter
    chips = n_row // 2
    row, rep = lax.axis_index("row"), lax.axis_index("rep")
    chip, core = lax.div(row, 2), lax.rem(row, 2)
    sibling = chip * 2 + 1 - core
    others = [lax.rem(chip + k, chips) * 2 + core for k in range(1, chips)]
    others_sib = [lax.rem(chip + k, chips) * 2 + 1 - core for k in range(1, chips)]
    reps = [lax.rem(rep + k, n_rep) for k in range(1, n_rep)]
    reps_from = [lax.rem(rep + n_rep - k, n_rep) for k in range(1, n_rep)]

    pending = []

    def local(src, dst, sem):
        copy = pltpu.make_async_copy(src, dst, local_sem.at[sem])
        copy.start()
        return copy

    tile_copy = local(tiles, tile_v, 0)
    own_copy = local(features, feat_v.at[pl.ds(row * per_block, per_block)], 2)
    w_copies = [
        local(src, dst, 3 + n)
        for n, (src, dst) in enumerate(
            (
                (self_one, w_one.at[pl.ds(0, width_in)]),
                (neigh_one, w_one.at[pl.ds(width_in, width_in)]),
                (self_two, w_self2),
                (neigh_two, w_neigh2),
            )
        )
    ]

    barrier = pltpu.get_barrier_semaphore()
    peers = [(r, rep) for r in others + [sibling]] + [(row, q) for q in reps]
    for peer in peers:
        pl.semaphore_signal(barrier, inc=1, device_id=peer, device_id_type=MESH)
    pl.semaphore_wait(barrier, len(peers))

    def remote(src, dst, send, recv, to):
        copy = pltpu.make_async_remote_copy(
            src_ref=src, dst_ref=dst, send_sem=send, recv_sem=recv, device_id=to, device_id_type=MESH
        )
        copy.start()
        pending.append(copy)
        return copy

    def arrived(ref, send, recv):
        pltpu.make_async_remote_copy(
            src_ref=ref, dst_ref=ref, send_sem=send, recv_sem=recv, device_id=(sibling, rep), device_id_type=MESH
        ).wait_recv()

    def feat_at(r):
        return feat_v.at[pl.ds(r * per_block, per_block)]

    for k, r in enumerate(others):
        remote(features, feat_at(row), f_send.at[k], f_recv.at[row], (r, rep))
    remote(features, feat_at(row), f_send.at[chips - 1], f_recv.at[row], (sibling, rep))
    for k, r in enumerate(others):
        arrived(feat_at(r), f_send.at[0], f_recv.at[r])
        remote(feat_at(r), feat_at(r), f_send.at[chips + k], f_recv.at[r], (sibling, rep))

    counts = jnp.broadcast_to(degree[pl.ds(rep, 1), :].astype(F32), (quarter, quarter))
    eye = lax.broadcasted_iota(jnp.int32, (quarter, quarter), 0) == lax.broadcasted_iota(
        jnp.int32, (quarter, quarter), 1
    )
    scale = jnp.sum(jnp.where(eye, counts, 0.0), axis=1, keepdims=True)
    own_copy.wait()
    tile_copy.wait()
    arrived(feat_at(sibling), f_send.at[0], f_recv.at[sibling])
    for r in others_sib:
        arrived(feat_at(r), f_send.at[0], f_recv.at[r])

    def product(held, start, width):
        acc[...] = jnp.zeros_like(acc)
        live_slots = jnp.full((1, width), count[0, 0], jnp.int32)

        def body(g, carry):
            lhs, rhs = [], []
            for u in range(GROUP):
                s = g * GROUP + u
                block = held[where[1, s], :, start : start + width]
                tile_row = jnp.full((1, width), where[0, s], jnp.int32)
                live = jnp.full((1, width), s, jnp.int32) < live_slots
                lhs.append(tile_v[s])
                rhs.append(
                    jnp.concatenate(
                        [
                            block * jnp.where(live & (tile_row == i), 1.0, 0.0).astype(BF16)
                            for i in range(per_block)
                        ],
                        axis=1,
                    )
                )
            acc[...] += jnp.dot(
                jnp.concatenate(lhs, axis=1), jnp.concatenate(rhs, axis=0), preferred_element_type=F32
            )
            return carry

        lax.fori_loop(0, slots // GROUP, body, 0)

    def send_partials(send, recv, send_sem, recv_sem, width):
        for q in range(n_rep):
            i, h = q // per_tile, q % per_tile
            part = acc[h * quarter : (h + 1) * quarter, i * width : (i + 1) * width]
            send[q] = part.astype(send.dtype)
        for k, q in enumerate(reps):
            remote(send.at[q], recv.at[k], send_sem.at[k], recv_sem.at[k], (row, q))

    def sum_partials(send, recv, send_sem, recv_sem):
        total = send[rep].astype(F32)
        for k in range(n_rep - 1):
            arrived(recv.at[k], send_sem.at[k], recv_sem.at[k])
            total += recv[k].astype(F32)
        return total

    def share_at(ref, r, q):
        start = pl.multiple_of(lax.rem(q, per_tile) * quarter, quarter)
        return ref.at[r * per_block + lax.div(q, per_tile), pl.ds(start, quarter)]

    product(feat_v, 0, width_in)
    send_partials(send1, recv1, p1_send, p1_recv, width_in)
    for copy in w_copies:
        copy.wait()
    total1 = sum_partials(send1, recv1, p1_send, p1_recv)
    share_at(agg_v, row, rep)[...] = (total1 / scale).astype(BF16)

    order = [rep] + reps_from
    for k, q in enumerate(reps):
        own = share_at(agg_v, row, rep)
        remote(own, own, h_send.at[0, k], h_recv.at[row, rep], (row, q))
    for n, q in enumerate(order):
        share = share_at(agg_v, row, q)
        if n:
            arrived(share, h_send.at[0, 0], h_recv.at[row, q])
        for k, r in enumerate(others):
            remote(share, share, h_send.at[1 + n, k], h_recv.at[row, q], (r, rep))
        remote(share, share, h_send.at[1 + n, chips - 1], h_recv.at[row, q], (sibling, rep))

    def hidden_of(r):
        for b in range(per_block):
            both = jnp.concatenate([feat_v[r * per_block + b], agg_v[r * per_block + b]], axis=1)
            first = jnp.dot(both, w_one[...], preferred_element_type=F32)
            hid_v[r * per_block + b] = jnp.maximum(first, 0.0).astype(BF16)

    hidden_of(row)
    for n, q in enumerate(order):
        for k, r in enumerate(others):
            share = share_at(agg_v, r, q)
            arrived(share, h_send.at[0, 0], h_recv.at[r, q])
            remote(share, share, h_send.at[1 + n, chips + k], h_recv.at[r, q], (sibling, rep))
    for r in others:
        hidden_of(r)
    for r in [sibling] + others_sib:
        for q in order:
            arrived(share_at(agg_v, r, q), h_send.at[0, 0], h_recv.at[r, q])
        hidden_of(r)

    parts = hid_v.shape[2] // width_in
    for c in range(parts):
        product(hid_v, c * width_in, width_in)
        send_partials(send2.at[c], recv2.at[c], p2_send.at[c], p2_recv.at[c], width_in)
    result = jnp.dot(share_at(hid_v, row, rep)[...], w_self2[...], preferred_element_type=F32)
    for c in range(parts):
        total2 = sum_partials(send2.at[c], recv2.at[c], p2_send.at[c], p2_recv.at[c])
        agg2 = (total2 / scale).astype(BF16)
        result += jnp.dot(
            agg2, w_neigh2[c * width_in : (c + 1) * width_in, :], preferred_element_type=F32
        )
    out_v[rep] = result.astype(BF16)
    for k, q in enumerate(reps):
        remote(out_v.at[rep], out_v.at[rep], o_send.at[k], o_recv.at[rep], (row, q))
    for q in reps_from:
        arrived(out_v.at[q], o_send.at[0], o_recv.at[q])
    for q in range(n_rep):
        out[q * quarter : (q + 1) * quarter, :] = out_v[q]
    for copy in pending:
        copy.wait_send()


def per_device(
    features, tiles, tile_where, tile_count, degree, self_one, neigh_one, self_two, neigh_two
):
    n_row, n_rep = lax.axis_size("row"), lax.axis_size("rep")
    rows, width_in = features.shape
    slots, _, tile, _ = tiles.shape
    hid, width_out = self_two.shape
    per_block = rows // tile
    quarter = rows // n_rep
    chips = n_row // 2
    parts = hid // width_in
    dma = pltpu.SemaphoreType.DMA
    any_spec = pl.BlockSpec(memory_space=pl.ANY)
    vmem = pl.BlockSpec(memory_space=pltpu.VMEM)
    out = pl.pallas_call(
        functools.partial(kernel, n_row, n_rep),
        out_shape=jax.ShapeDtypeStruct((rows, width_out), BF16),
        in_specs=[pl.BlockSpec(memory_space=pltpu.SMEM)] * 2 + [vmem] + [any_spec] * 6,
        out_specs=vmem,
        scratch_shapes=[
            pltpu.VMEM((slots, tile, tile), BF16),
            pltpu.VMEM((n_row * per_block, tile, width_in), BF16),
            pltpu.VMEM((2 * width_in, hid), BF16),
            pltpu.VMEM(self_two.shape, BF16),
            pltpu.VMEM(neigh_two.shape, BF16),
            pltpu.VMEM((tile, per_block * width_in), F32),
            pltpu.VMEM((n_rep, quarter, width_in), F32),
            pltpu.VMEM((n_rep - 1, quarter, width_in), F32),
            pltpu.VMEM((n_row * per_block, tile, width_in), BF16),
            pltpu.VMEM((n_row * per_block, tile, hid), BF16),
            pltpu.VMEM((parts, n_rep, quarter, width_in), BF16),
            pltpu.VMEM((parts, n_rep - 1, quarter, width_in), BF16),
            pltpu.VMEM((n_rep, quarter, width_out), BF16),
            dma((7,)),
            dma((2 * chips,)),
            dma((n_row,)),
            dma((n_rep - 1,)),
            dma((n_rep - 1,)),
            dma((1 + n_rep, max(2 * chips, n_rep))),
            dma((n_row, n_rep)),
            dma((parts, n_rep - 1)),
            dma((parts, n_rep - 1)),
            dma((n_rep - 1,)),
            dma((n_rep,)),
        ],
        compiler_params=pltpu.CompilerParams(
            collective_id=0, has_side_effects=True, vmem_limit_bytes=56 * 1024 * 1024
        ),
        name="sage",
    )(
        tile_where.reshape(slots, 2).T, tile_count, degree.reshape(n_rep, quarter), features.reshape(per_block, tile, width_in), tiles.reshape(slots, tile, tile),
        self_one, neigh_one, self_two, neigh_two,
    )
    return out.astype(F32)


def solution(mesh):
    return jax.shard_map(
        per_device,
        mesh=mesh,
        in_specs=(
            P("row", None),
            P("row", "rep", None, None),
            P("row", "rep", None),
            P("row", "rep"),
            P("row"),
            P(),
            P(),
            P(),
            P(),
        ),
        out_specs=P("row", None),
        check_vma=False,
    )
```

```python
import functools

import jax
import jax.numpy as jnp
from jax import lax
from jax.experimental import pallas as pl
from jax.experimental.pallas import tpu as pltpu
from jax.sharding import PartitionSpec as P

GROUP = 8
MESH = pl.DeviceIdType.MESH
F32 = jnp.float32
BF16 = jnp.bfloat16


def kernel(
    n_row, n_rep, dense,
    where, count, table, degree, features, tiles, self_one, neigh_one, self_two, neigh_two,
    out,
    tile_v, feat_v, w_one, w_self2, w_neigh2,
    acc, send1, recv1, agg_v, hid_v, cell_v, acc2, send2, recv2, out_v,
    local_sem, f_send, f_recv, p1_send, p1_recv, h_send, h_recv, p2_send, p2_recv, o_send, o_recv,
):
    slots, tile, _ = tile_v.shape
    per_block, _, width_in = features.shape
    rows = per_block * tile
    quarter = rows // n_rep
    per_tile = tile // quarter
    chips = n_row // 2
    row, rep = lax.axis_index("row"), lax.axis_index("rep")
    chip, core = lax.div(row, 2), lax.rem(row, 2)
    sibling = chip * 2 + 1 - core
    others = [lax.rem(chip + k, chips) * 2 + core for k in range(1, chips)]
    others_sib = [lax.rem(chip + k, chips) * 2 + 1 - core for k in range(1, chips)]
    reps = [lax.rem(rep + k, n_rep) for k in range(1, n_rep)]
    reps_from = [lax.rem(rep + n_rep - k, n_rep) for k in range(1, n_rep)]

    pending = []

    def local(src, dst, sem):
        copy = pltpu.make_async_copy(src, dst, local_sem.at[sem])
        copy.start()
        return copy

    tile_copy = local(tiles, tile_v, 0)
    own_copy = local(features, feat_v.at[pl.ds(row * per_block, per_block)], 2)
    w_copies = [
        local(src, dst, 3 + n)
        for n, (src, dst) in enumerate(
            (
                (self_one, w_one.at[pl.ds(0, width_in)]),
                (neigh_one, w_one.at[pl.ds(width_in, width_in)]),
                (self_two, w_self2),
                (neigh_two, w_neigh2),
            )
        )
    ]

    barrier = pltpu.get_barrier_semaphore()
    peers = [(r, rep) for r in others + [sibling]] + [(row, q) for q in reps]
    for peer in peers:
        pl.semaphore_signal(barrier, inc=1, device_id=peer, device_id_type=MESH)
    pl.semaphore_wait(barrier, len(peers))

    def remote(src, dst, send, recv, to):
        copy = pltpu.make_async_remote_copy(
            src_ref=src, dst_ref=dst, send_sem=send, recv_sem=recv, device_id=to, device_id_type=MESH
        )
        copy.start()
        pending.append(copy)
        return copy

    def arrived(ref, send, recv):
        pltpu.make_async_remote_copy(
            src_ref=ref, dst_ref=ref, send_sem=send, recv_sem=recv, device_id=(sibling, rep), device_id_type=MESH
        ).wait_recv()

    def build_cells():
        chunk = min(64, tile)
        cell_v[slots] = jnp.zeros((tile, tile), BF16)
        for start in range(0, tile, chunk):

            def body(g, run):
                for u in range(GROUP):
                    k = g * GROUP + u
                    piece = tile_v[table[0, k], start : start + chunk, :].astype(F32)
                    run = run * jnp.full((1, tile), table[1, k], jnp.int32).astype(F32) + piece
                    cell_v[k, start : start + chunk, :] = run.astype(BF16)
                return run

            lax.fori_loop(0, slots // GROUP, body, jnp.zeros((chunk, tile), F32))

    def feat_at(r):
        return feat_v.at[pl.ds(r * per_block, per_block)]

    for k, r in enumerate(others):
        remote(features, feat_at(row), f_send.at[k], f_recv.at[row], (r, rep))
    remote(features, feat_at(row), f_send.at[chips - 1], f_recv.at[row], (sibling, rep))
    if dense:
        tile_copy.wait()
        build_cells()
    for k, r in enumerate(others):
        arrived(feat_at(r), f_send.at[0], f_recv.at[r])
        remote(feat_at(r), feat_at(r), f_send.at[chips + k], f_recv.at[r], (sibling, rep))

    counts = jnp.broadcast_to(degree[pl.ds(rep, 1), :].astype(F32), (quarter, quarter))
    eye = lax.broadcasted_iota(jnp.int32, (quarter, quarter), 0) == lax.broadcasted_iota(
        jnp.int32, (quarter, quarter), 1
    )
    scale = jnp.sum(jnp.where(eye, counts, 0.0), axis=1, keepdims=True)
    own_copy.wait()
    if not dense:
        tile_copy.wait()
    arrived(feat_at(sibling), f_send.at[0], f_recv.at[sibling])
    for r in others_sib:
        arrived(feat_at(r), f_send.at[0], f_recv.at[r])

    def product(held, start, width):
        acc[...] = jnp.zeros_like(acc)
        live_slots = jnp.full((1, width), count[0, 0], jnp.int32)

        def body(g, carry):
            lhs, rhs = [], []
            for u in range(GROUP):
                s = g * GROUP + u
                block = held[where[1, s], :, start : start + width]
                tile_row = jnp.full((1, width), where[0, s], jnp.int32)
                live = jnp.full((1, width), s, jnp.int32) < live_slots
                lhs.append(tile_v[s])
                rhs.append(
                    jnp.concatenate(
                        [
                            block * jnp.where(live & (tile_row == i), 1.0, 0.0).astype(BF16)
                            for i in range(per_block)
                        ],
                        axis=1,
                    )
                )
            acc[...] += jnp.dot(
                jnp.concatenate(lhs, axis=1), jnp.concatenate(rhs, axis=0), preferred_element_type=F32
            )
            return carry

        lax.fori_loop(0, slots // GROUP, body, 0)

    def send_partials(send, recv, send_sem, recv_sem, width, start=None):
        for q in range(n_rep):
            i, h = q // per_tile, q % per_tile
            if start is None:
                part = acc[h * quarter : (h + 1) * quarter, i * width : (i + 1) * width]
            else:
                part = acc2[i, h * quarter : (h + 1) * quarter, start : start + width]
            send[q] = part.astype(send.dtype)
        for k, q in enumerate(reps):
            remote(send.at[q], recv.at[k], send_sem.at[k], recv_sem.at[k], (row, q))

    def sum_partials(send, recv, send_sem, recv_sem):
        total = send[rep].astype(F32)
        for k in range(n_rep - 1):
            arrived(recv.at[k], send_sem.at[k], recv_sem.at[k])
            total += recv[k].astype(F32)
        return total

    def share_at(ref, r, q):
        start = pl.multiple_of(lax.rem(q, per_tile) * quarter, quarter)
        return ref.at[r * per_block + lax.div(q, per_tile), pl.ds(start, quarter)]

    product(feat_v, 0, width_in)
    send_partials(send1, recv1, p1_send, p1_recv, width_in)
    for copy in w_copies:
        copy.wait()
    total1 = sum_partials(send1, recv1, p1_send, p1_recv)
    share_at(agg_v, row, rep)[...] = (total1 / scale).astype(BF16)

    order = [rep] + reps_from
    for k, q in enumerate(reps):
        own = share_at(agg_v, row, rep)
        remote(own, own, h_send.at[0, k], h_recv.at[row, rep], (row, q))
    for n, q in enumerate(order):
        share = share_at(agg_v, row, q)
        if n:
            arrived(share, h_send.at[0, 0], h_recv.at[row, q])
        for k, r in enumerate(others):
            remote(share, share, h_send.at[1 + n, k], h_recv.at[row, q], (r, rep))
        remote(share, share, h_send.at[1 + n, chips - 1], h_recv.at[row, q], (sibling, rep))

    def hidden_of(r):
        for b in range(per_block):
            both = jnp.concatenate([feat_v[r * per_block + b], agg_v[r * per_block + b]], axis=1)
            first = jnp.dot(both, w_one[...], preferred_element_type=F32)
            hid_v[r * per_block + b] = jnp.maximum(first, 0.0).astype(BF16)
        if dense:
            columns = n_row * per_block
            lhs = jnp.concatenate(
                [
                    jnp.concatenate(
                        [cell_v[table[2, i * columns + r * per_block + b]] for b in range(per_block)], axis=1
                    )
                    for i in range(per_block)
                ],
                axis=0,
            )
            rhs = jnp.concatenate([hid_v[r * per_block + b] for b in range(per_block)], axis=0)
            step = jnp.dot(lhs, rhs, preferred_element_type=F32)
            for i in range(per_block):
                acc2[i] += step[i * tile : (i + 1) * tile]

    acc2[...] = jnp.zeros_like(acc2)
    hidden_of(row)
    for n, q in enumerate(order):
        for k, r in enumerate(others):
            share = share_at(agg_v, r, q)
            arrived(share, h_send.at[0, 0], h_recv.at[r, q])
            remote(share, share, h_send.at[1 + n, chips + k], h_recv.at[r, q], (sibling, rep))
    for r in others:
        hidden_of(r)
    for r in [sibling] + others_sib:
        for q in order:
            arrived(share_at(agg_v, r, q), h_send.at[0, 0], h_recv.at[r, q])
        hidden_of(r)

    parts = hid_v.shape[2] // width_in
    for c in range(parts):
        if not dense:
            product(hid_v, c * width_in, width_in)
        send_partials(
            send2.at[c], recv2.at[c], p2_send.at[c], p2_recv.at[c], width_in, c * width_in if dense else None
        )
    result = jnp.dot(share_at(hid_v, row, rep)[...], w_self2[...], preferred_element_type=F32)
    for c in range(parts):
        total2 = sum_partials(send2.at[c], recv2.at[c], p2_send.at[c], p2_recv.at[c])
        agg2 = (total2 / scale).astype(BF16)
        result += jnp.dot(
            agg2, w_neigh2[c * width_in : (c + 1) * width_in, :], preferred_element_type=F32
        )
    out_v[rep] = result.astype(BF16)
    for k, q in enumerate(reps):
        remote(out_v.at[rep], out_v.at[rep], o_send.at[k], o_recv.at[rep], (row, q))
    for q in reps_from:
        arrived(out_v.at[q], o_send.at[0], o_recv.at[q])
    for q in range(n_rep):
        out[q * quarter : (q + 1) * quarter, :] = out_v[q]
    for copy in pending:
        copy.wait_send()


def order_kernel(columns, cells, count, where, table):
    slots = where.shape[1]

    def total(cond, value, axis):
        return jnp.sum(jnp.where(cond, value, 0.0), axis=axis, keepdims=True)

    square = (slots, slots)
    sub = lax.broadcasted_iota(jnp.int32, square, 0)
    lane = lax.broadcasted_iota(jnp.int32, square, 1)
    spread = jnp.broadcast_to(where[0:1, :] * columns + where[1:2, :], square)
    of_lane = jnp.where(lane < jnp.full(square, count[0, 0], jnp.int32), spread, cells).astype(F32)
    of_sub = total(lane == sub, of_lane, 1)
    earlier = (of_lane == of_sub) & (lane < sub)
    rank = total((of_lane < of_sub) | earlier, 1.0, 1)
    seen = total(earlier, 1.0, 1)
    hit = rank == lane.astype(F32)
    table[0:1, 0:slots] = total(hit, sub.astype(F32), 0).astype(jnp.int32)
    table[1:2, 0:slots] = total(hit & (seen > 0.0), 1.0, 0).astype(jnp.int32)
    cell = lax.broadcasted_iota(jnp.int32, (slots, cells), 1).astype(F32)
    upto = total(of_sub <= cell, 1.0, 0)
    here = total(of_sub == cell, 1.0, 0)
    table[2:3, 0:cells] = jnp.where(here > 0.0, upto - 1.0, float(slots)).astype(jnp.int32)


def per_device(
    features, tiles, tile_where, tile_count, degree, self_one, neigh_one, self_two, neigh_two
):
    n_row, n_rep = lax.axis_size("row"), lax.axis_size("rep")
    rows, width_in = features.shape
    slots, _, tile, _ = tiles.shape
    hid, width_out = self_two.shape
    per_block = rows // tile
    quarter = rows // n_rep
    chips = n_row // 2
    parts = hid // width_in
    columns = n_row * per_block
    cells = per_block * columns
    dense = cells <= slots
    where = tile_where.reshape(slots, 2).T
    smem = pl.BlockSpec(memory_space=pltpu.SMEM)
    if dense:
        table = pl.pallas_call(
            functools.partial(order_kernel, columns, cells),
            out_shape=jax.ShapeDtypeStruct((3, max(slots, cells)), jnp.int32),
            in_specs=[smem, pl.BlockSpec(memory_space=pltpu.VMEM)],
            out_specs=pl.BlockSpec(memory_space=pltpu.VMEM),
            name="order",
        )(tile_count, where)
    else:
        table = where
    dma = pltpu.SemaphoreType.DMA
    any_spec = pl.BlockSpec(memory_space=pl.ANY)
    vmem = pl.BlockSpec(memory_space=pltpu.VMEM)
    out = pl.pallas_call(
        functools.partial(kernel, n_row, n_rep, dense),
        out_shape=jax.ShapeDtypeStruct((rows, width_out), BF16),
        in_specs=[smem] * 3 + [vmem] + [any_spec] * 6,
        out_specs=vmem,
        scratch_shapes=[
            pltpu.VMEM((slots, tile, tile), BF16),
            pltpu.VMEM((n_row * per_block, tile, width_in), BF16),
            pltpu.VMEM((2 * width_in, hid), BF16),
            pltpu.VMEM(self_two.shape, BF16),
            pltpu.VMEM(neigh_two.shape, BF16),
            pltpu.VMEM((tile, per_block * width_in), F32),
            pltpu.VMEM((n_rep, quarter, width_in), F32),
            pltpu.VMEM((n_rep - 1, quarter, width_in), F32),
            pltpu.VMEM((n_row * per_block, tile, width_in), BF16),
            pltpu.VMEM((n_row * per_block, tile, hid), BF16),
            pltpu.VMEM((slots + 1 if dense else 1, tile, tile), BF16),
            pltpu.VMEM((per_block, tile, hid), F32),
            pltpu.VMEM((parts, n_rep, quarter, width_in), BF16),
            pltpu.VMEM((parts, n_rep - 1, quarter, width_in), BF16),
            pltpu.VMEM((n_rep, quarter, width_out), BF16),
            dma((7,)),
            dma((2 * chips,)),
            dma((n_row,)),
            dma((n_rep - 1,)),
            dma((n_rep - 1,)),
            dma((1 + n_rep, max(2 * chips, n_rep))),
            dma((n_row, n_rep)),
            dma((parts, n_rep - 1)),
            dma((parts, n_rep - 1)),
            dma((n_rep - 1,)),
            dma((n_rep,)),
        ],
        compiler_params=pltpu.CompilerParams(
            collective_id=0, has_side_effects=True, vmem_limit_bytes=56 * 1024 * 1024
        ),
        name="sage",
    )(
        where, tile_count, table, degree.reshape(n_rep, quarter), features.reshape(per_block, tile, width_in), tiles.reshape(slots, tile, tile),
        self_one, neigh_one, self_two, neigh_two,
    )
    return out.astype(F32)


def solution(mesh):
    return jax.shard_map(
        per_device,
        mesh=mesh,
        in_specs=(
            P("row", None),
            P("row", "rep", None, None),
            P("row", "rep", None),
            P("row", "rep"),
            P("row"),
            P(),
            P(),
            P(),
            P(),
        ),
        out_specs=P("row", None),
        check_vma=False,
    )
```
